512 devices in a mesh: row: 32 (over y, x), col: 16 (over z, core).
Axes of the slice: x: 4, y: 8, z: 8, core: 2. Of those that a mesh axis runs over, the one named last changes fastest.
Arguments:
- matrix: float32 [16384, 16384], P('row', 'col'), as said below
- reflectors: float32 [16384, 256], P('row'), may hold values from -0.046875 to 0.046875
Outputs:
- updated: float32 [16384, 16384], P('row', 'col')
The draws below stay inside these ranges and needn't reach their ends.
Inputs may be any that keep to these rules, and one draw needn't show every extreme that they name: matrix is exactly symmetric.
All inputs are finite; a program needn't handle non-finite values.
Results may differ from the reference program's by a relative error of at most 0.0001.
Values sent between devices are 32-bit elements; how exact they have to be, the bound alone decides.
A program may use at most 64 MiB of HBM per device.

```python
import jax
import jax.numpy as jnp
from jax import lax

N = 16384
NB = 256


def draw_matrix(key, part):
    key = jax.random.fold_in(key, 7)
    base = jax.random.normal(key, (N, N), jnp.float32)
    return (base + base.T) * 0.7071


def steps_of(own_key, dims, pieces, least, high):
    loudness = 1.0
    for position, shards_of in pieces:
        heights = jax.random.uniform(jax.random.fold_in(jax.random.fold_in(own_key, 6), position), (shards_of,), jnp.float32, least / len(pieces), high / len(pieces))
        loudness = loudness * jnp.repeat(jnp.exp(heights), dims[position] // shards_of).reshape((-1,) + (1,) * (len(dims) - 1 - position))
    return loudness


def centred(own_key, shape, deviation, most, shards=(), kind=jnp.bfloat16):
    values = jax.random.normal(own_key, shape, jnp.float32) * deviation
    if len(shards) > 0:
        values = steps_of(own_key, shape, shards, -0.22, 0.18) * values
    return jnp.clip(values, min=-most, max=most).astype(kind)


def setup_inputs(seed: int = 0) -> dict:
    key_list = jax.random.split(jax.random.key(seed), 3)
    return {
        "matrix": draw_matrix(jax.random.fold_in(key_list[2], 71), 0),
        "reflectors": centred(key_list[1], (N, NB), N ** -0.5, 0.046875, ((0, 32),), jnp.float32),
    }


def full_dot(left, right):
    return jnp.dot(left, right, precision=lax.Precision.HIGHEST, preferred_element_type=jnp.float32)


def invert_upper(upper, width):
    inv_diag = 1.0 / jnp.diag(upper)
    ident = jnp.eye(width, dtype=jnp.float32)
    strict = jnp.triu(upper, 1) * inv_diag[:, None]
    result = ident - strict
    power = full_dot(strict, strict)
    span = 2
    while span < width:
        result = full_dot(result, ident + power)
        power = full_dot(power, power)
        span = span * 2
    return result * inv_diag[None, :]


def reference(matrix, reflectors):
    row_index = jnp.arange(N, dtype=jnp.int32)[:, None]
    col_index = jnp.arange(NB, dtype=jnp.int32)[None, :]
    lead = col_index + NB
    vecs = jnp.where(row_index > lead, reflectors, jnp.where(row_index == lead, jnp.float32(1.0), jnp.float32(0.0)))
    gram = full_dot(vecs.T, vecs)
    upper = jnp.triu(gram) - 0.5 * jnp.diag(jnp.diag(gram))
    tfac = invert_upper(upper, NB)
    prod = full_dot(matrix, vecs)
    yblk = full_dot(prod, tfac)
    small = full_dot(full_dot(tfac.T, full_dot(vecs.T, prod)), tfac)
    zblk = yblk - 0.5 * full_dot(vecs, small)
    return matrix - full_dot(vecs, zblk.T) - full_dot(zblk, vecs.T)
```

```python
import jax
import jax.numpy as jnp
from jax import lax
from jax.experimental import pallas as pl
from jax.experimental.pallas import tpu as pltpu
from jax.sharding import PartitionSpec as P

MESH = pl.DeviceIdType.MESH
F32 = jnp.float32
BF16 = jnp.bfloat16
NX, NY, NZ = 4, 8, 8
RB, CB, NB = 512, 1024, 256
SL = RB // 16
GS = NB // 16
NG = 4
GR = RB // NG


def split(value):
    high = value.astype(BF16)
    return high, (value - high.astype(F32)).astype(BF16)


def dims(left, right):
    return (((left,), (right,)), ((), ()))


def dot_split(left, right, contract):
    (lh, ll), (rh, rl) = left, right
    out = lax.dot_general(lh, rl, contract, preferred_element_type=F32)
    out += lax.dot_general(ll, rh, contract, preferred_element_type=F32)
    out += lax.dot_general(lh, rh, contract, preferred_element_type=F32)
    return out


def dot_full(left, right, contract):
    return lax.dot_general(
        left, right, contract, precision=lax.Precision.HIGHEST, preferred_element_type=F32
    )


NN, NT, TN = dims(1, 0), dims(1, 1), dims(0, 0)


def device(x, y, z, k):
    return (y * NX + x, z * 2 + k)


def kernel(
    a_ref,
    v_ref,
    o_ref,
    vm,
    vcol,
    ah,
    al,
    vch,
    vcl,
    ppart,
    swapb,
    psum,
    rsb,
    prow,
    pcol,
    gloc,
    gram,
    gx,
    gy,
    sx,
    sy,
    sloc,
    smat,
    res,
    powr,
    lh,
    ll,
    rh,
    rl,
    v_send,
    v_recv,
    vf_send,
    p_send,
    p_recv,
    pf_send,
    sw_send,
    sw_recv,
    rs_send,
    rs_recv,
    pr_send,
    pr_recv,
    gx_send,
    gx_recv,
    gy_send,
    gy_recv,
    gz_send,
    gz_recv,
    gc_sem,
    sx_send,
    sx_recv,
    sy_send,
    sy_recv,
    sz_send,
    sz_recv,
    sc_sem,
):
    grow = lax.axis_index("row")
    gcol = lax.axis_index("col")
    x, y, z, k = grow % NX, grow // NX, gcol // 2, gcol % 2
    kx = x // 2
    hub = k == kx
    mine = 8 * k + z
    twin = device(x, y, z, 1 - k)

    def remote(src, dst, send, recv, target):
        return pltpu.make_async_remote_copy(
            src_ref=src,
            dst_ref=dst,
            send_sem=send,
            recv_sem=recv,
            device_id=target,
            device_id_type=MESH,
        )

    barrier = pltpu.get_barrier_semaphore()

    def greet(target):
        pl.semaphore_signal(barrier, inc=1, device_id=target, device_id_type=MESH)

    for d in range(1, NX):
        greet(device((x + d) % NX, y, z, k))
    for d in range(1, NY):
        greet(device(x, (y + d) % NY, z, k))
    for d in range(1, NZ):
        greet(device(x, y, (z + d) % NZ, k))
    greet(twin)

    @pl.when(hub)
    def _():
        for d in range(NZ):
            for e in range(2):
                zz = (z + d) % NZ
                if d == 0:

                    @pl.when(jnp.logical_not(jnp.logical_and(y == z, k == e)))
                    def _():
                        greet(device(x, z, zz, e))
                else:
                    greet(device(x, z, zz, e))

    has_self = jnp.logical_and(z == y, hub)
    others = 3 + 7 + 7 + 1 + 8
    pl.semaphore_wait(barrier, others - jnp.where(has_self, 1, 0))

    def spread(src, dst, send, recv, start):
        for d in range(NY):
            place = dst.at[pl.ds(RB * (x % 2) + SL * mine, SL)]
            sem = recv.at[x % 2, mine // 4]
            cp = remote(src, place, send.at[d], sem, device(x, (y + d) % NY, y, kx))
            if d == 0:

                @pl.when(has_self)
                def _():
                    if start:
                        pltpu.make_async_copy(src, place, sem).start()

                @pl.when(jnp.logical_not(has_self))
                def _():
                    if start:
                        cp.start()
                    else:
                        cp.wait_send()
            elif start:
                cp.start()
            else:
                cp.wait_send()

    def group(ref, j, g):
        return ref.at[pl.ds(RB * j + GR * g, GR)]

    def await_group(ref, recv, j, g):
        part = group(ref, j, g)
        pltpu.make_async_copy(part, part, recv.at[j, g]).wait()

    def forward(ref, send, recv, g, d, start):
        part = group(ref, x % 2, g)
        cp = remote(
            part, part, send.at[d - 1, g], recv.at[x % 2, g], device((x + d) % NX, y, z, k)
        )
        if start:
            cp.start()
        else:
            cp.wait_send()

    def forward_all(ref, send, recv):
        @pl.when(hub)
        def _():
            def step(i, carry):
                g = (i + 2 * k + z // 4) % NG
                await_group(ref, recv, x % 2, g)
                for d in (1, 3, 2):
                    forward(ref, send, recv, g, d, True)
                return carry

            lax.fori_loop(0, NG, step, 0)

    def await_rest(ref, recv):
        for j in range(2):

            @pl.when(jnp.logical_not(jnp.logical_and(hub, x % 2 == j)))
            def _():
                for g in range(NG):
                    await_group(ref, recv, j, g)

    def finish_forward(ref, send, recv):
        @pl.when(hub)
        def _():
            for g in range(NG):
                for d in (1, 2, 3):
                    forward(ref, send, recv, g, d, False)

    def lined(buf, own, size, send, recv, count, make, start):
        for d in range(1, count):
            part = buf.at[pl.ds(own * size, size)]
            cp = remote(part, part, send.at[d], recv.at[own], make(d))
            if start:
                cp.start()
            else:
                cp.wait_send()

    def await_line(buf, own, size, recv, count):
        for d in range(1, count):
            other = (own + d) % count
            part = buf.at[pl.ds(other * size, size)]
            pltpu.make_async_copy(part, part, recv.at[other]).wait()

    x_line = lambda d: device((x + d) % NX, y, z, k)
    y_line = lambda d: device(x, (y + d) % NY, z, k)
    z_line = lambda d: device(x, y, (z + d) % NZ, k)

    spread(v_ref.at[pl.ds(SL * mine, SL)], vcol, v_send, v_recv, True)

    def masked(value, first):
        rows = first + lax.broadcasted_iota(jnp.int32, value.shape, 0)
        lead = NB + lax.broadcasted_iota(jnp.int32, value.shape, 1)
        return jnp.where(rows > lead, value, jnp.where(rows == lead, 1.0, 0.0).astype(F32))

    vm[...] = masked(v_ref[...], grow * RB)
    gloc[...] = dot_full(vm[...], vm[...], TN)
    gx[pl.ds(x * GS, GS)] = gloc[pl.ds(mine * GS, GS)]
    lined(gx, x, GS, gx_send, gx_recv, NX, x_line, True)

    forward_all(vcol, vf_send, v_recv)

    def split_a(i, carry):
        rows = pl.ds(pl.multiple_of(i * 64, 64), 64)
        high, low = split(a_ref[rows])
        ah[rows] = high
        al[rows] = low
        return carry

    lax.fori_loop(0, RB // 64, split_a, 0)

    def fold(buf, count, size):
        total = buf[pl.ds(0, size)]
        for i in range(1, count):
            total = total + buf[pl.ds(i * size, size)]
        return total

    await_line(gx, x, GS, gx_recv, NX)
    gy[pl.ds(y * GS, GS)] = fold(gx, NX, GS)
    lined(gy, y, GS, gy_send, gy_recv, NY, y_line, True)

    await_rest(vcol, v_recv)

    vcm = masked(vcol[...], gcol * CB)
    high, low = split(vcm)
    vch[...] = high
    vcl[...] = low

    def part_p(first):
        def step(i, carry):
            rows = pl.ds(pl.multiple_of(first + i * 128, 128), 128)
            ppart[rows] = dot_split((ah[rows], al[rows]), (vch[...], vcl[...]), NN)
            return carry

        lax.fori_loop(0, 2, step, 0)

    half = RB // 2
    part_p((1 - k) * half)
    swap = remote(ppart.at[pl.ds((1 - k) * half, half)], swapb, sw_send.at[0], sw_recv.at[0], twin)
    swap.start()
    part_p(k * half)

    await_line(gy, y, GS, gy_recv, NY)
    gram[pl.ds(mine * GS, GS)] = fold(gy, NY, GS)
    lined_g = [
        remote(
            gram.at[pl.ds(mine * GS, GS)],
            gram.at[pl.ds(mine * GS, GS)],
            gz_send.at[d],
            gz_recv.at[z],
            z_line(d),
        )
        for d in range(1, NZ)
    ]

    swap.wait_recv()
    psum[...] = ppart[pl.ds(k * half, half)] + swapb[...]
    rs = []
    for d in range(1, NZ):
        zz = (z + d) % NZ
        cp = remote(psum.at[pl.ds(zz * SL, SL)], rsb.at[z], rs_send.at[d], rs_recv.at[z], z_line(d))
        cp.start()
        rs.append(cp)
    for cp in lined_g:
        cp.start()

    def await_z(buf, size, recv):
        for d in range(1, NZ):
            other = (z + d) % NZ
            part = buf.at[pl.ds((8 * k + other) * size, size)]
            pltpu.make_async_copy(part, part, recv.at[other]).wait()

    await_z(gram, GS, gz_recv)
    ghalf = gram.at[pl.ds(k * 128, 128)]
    gtwin = remote(ghalf, ghalf, gc_sem.at[0], gc_sem.at[1], twin)
    gtwin.start()

    for d in range(1, NZ):
        zz = (z + d) % NZ
        pltpu.make_async_copy(rsb.at[zz], rsb.at[zz], rs_recv.at[zz]).wait()
    total = psum[pl.ds(z * SL, SL)]
    for d in range(1, NZ):
        total = total + rsb[(z + d) % NZ]
    own_rows = pl.ds(mine * SL, SL)
    prow[own_rows] = total

    spread(prow.at[own_rows], pcol, p_send, p_recv, True)
    pr = [
        remote(prow.at[own_rows], prow.at[own_rows], pr_send.at[d], pr_recv.at[z], z_line(d))
        for d in range(1, NZ)
    ]
    for cp in pr:
        cp.start()

    ghalf2 = gram.at[pl.ds((1 - k) * 128, 128)]
    pltpu.make_async_copy(ghalf2, ghalf2, gc_sem.at[1]).wait()
    ri = lax.broadcasted_iota(jnp.int32, (NB, NB), 0)
    ci = lax.broadcasted_iota(jnp.int32, (NB, NB), 1)
    ident = jnp.where(ri == ci, 1.0, 0.0).astype(F32)
    full = gram[...]
    diag = jnp.where(ri == ci, full, 0.0) * 0.5
    inv_col = 1.0 / jnp.sum(diag, axis=1, keepdims=True)
    inv_row = 1.0 / jnp.sum(diag, axis=0, keepdims=True)
    strict = jnp.where(ri < ci, full, 0.0) * inv_col
    res[...] = ident - strict
    powr[...] = dot_full(strict, strict, NN)

    forward_all(pcol, pf_send, p_recv)

    def grow_inverse(i, carry):
        power = powr[...]
        res[...] += dot_full(res[...], power, NN)
        powr[...] = dot_full(power, power, NN)
        return carry

    lax.fori_loop(0, 7, grow_inverse, 0)

    await_z(prow, SL, pr_recv)
    phalf = prow.at[pl.ds(k * half, half)]
    ptwin = remote(phalf, phalf, sw_send.at[1], sw_recv.at[1], twin)
    ptwin.start()

    tfac = split(res[...] * inv_row)
    wide = dot_split(split(vm[...]), tfac, NT)
    high, low = split(wide)
    lh[:, 0:NB] = high
    ll[:, 0:NB] = low

    phalf2 = prow.at[pl.ds((1 - k) * half, half)]
    pltpu.make_async_copy(phalf2, phalf2, sw_recv.at[1]).wait()

    sloc[...] = dot_split(split(vm[...]), split(prow[...]), TN)
    sx[pl.ds(x * GS, GS)] = sloc[pl.ds(mine * GS, GS)]
    lined(sx, x, GS, sx_send, sx_recv, NX, x_line, True)

    def wide_cols(i, carry):
        rows = pl.ds(pl.multiple_of(i * 256, 256), 256)
        w = dot_split((vch[rows], vcl[rows]), tfac, NT)
        high, low = split(w)
        rh[rows, NB:] = high
        rl[rows, NB:] = low
        return carry

    lax.fori_loop(0, CB // 256, wide_cols, 0)

    await_line(sx, x, GS, sx_recv, NX)
    sy[pl.ds(y * GS, GS)] = fold(sx, NX, GS)
    lined(sy, y, GS, sy_send, sy_recv, NY, y_line, True)

    await_rest(pcol, p_recv)

    def split_pc(i, carry):
        rows = pl.ds(pl.multiple_of(i * 256, 256), 256)
        high, low = split(pcol[rows])
        rh[rows, 0:NB] = high
        rl[rows, 0:NB] = low
        return carry

    lax.fori_loop(0, CB // 256, split_pc, 0)

    await_line(sy, y, GS, sy_recv, NY)
    smat[pl.ds(mine * GS, GS)] = fold(sy, NY, GS)
    own_s = smat.at[pl.ds(mine * GS, GS)]
    lined_s = [remote(own_s, own_s, sz_send.at[d], sz_recv.at[z], z_line(d)) for d in range(1, NZ)]
    for cp in lined_s:
        cp.start()

    def first_part(i, carry):
        rows = pl.ds(pl.multiple_of(i * 128, 128), 128)
        o_ref[rows] = a_ref[rows] - dot_split(
            (lh[rows, 0:NB], ll[rows, 0:NB]), (rh[:, 0:NB], rl[:, 0:NB]), NT
        )
        return carry

    lax.fori_loop(0, 4, first_part, 0)

    await_z(smat, GS, sz_recv)
    shalf = smat.at[pl.ds(k * 128, 128)]
    stwin = remote(shalf, shalf, sc_sem.at[0], sc_sem.at[1], twin)
    stwin.start()
    shalf2 = smat.at[pl.ds((1 - k) * 128, 128)]
    pltpu.make_async_copy(shalf2, shalf2, sc_sem.at[1]).wait()

    ssplit = split(smat[...])
    rest = prow[...] - dot_split((lh[:, 0:NB], ll[:, 0:NB]), ssplit, NN)
    high, low = split(rest)
    lh[:, NB:] = high
    ll[:, NB:] = low

    def last_part(i, carry):
        rows = pl.ds(pl.multiple_of(i * 128, 128), 128)
        o_ref[rows] = o_ref[rows] - dot_split(
            (lh[rows, NB:], ll[rows, NB:]), (rh[:, NB:], rl[:, NB:]), NT
        )
        return carry

    lax.fori_loop(0, 4, last_part, 0)

    spread(v_ref.at[pl.ds(SL * mine, SL)], vcol, v_send, v_recv, False)
    spread(prow.at[own_rows], pcol, p_send, p_recv, False)
    finish_forward(vcol, vf_send, v_recv)
    finish_forward(pcol, pf_send, p_recv)
    lined(gx, x, GS, gx_send, gx_recv, NX, x_line, False)
    lined(gy, y, GS, gy_send, gy_recv, NY, y_line, False)
    lined(sx, x, GS, sx_send, sx_recv, NX, x_line, False)
    lined(sy, y, GS, sy_send, sy_recv, NY, y_line, False)
    for cp in [swap, gtwin, ptwin, stwin] + rs + lined_g + pr + lined_s:
        cp.wait_send()


def per_device(matrix, reflectors):
    vmem = lambda shape, kind=F32: pltpu.VMEM(shape, kind)
    dma = lambda *shape: pltpu.SemaphoreType.DMA(shape)
    return pl.pallas_call(
        kernel,
        out_shape=jax.ShapeDtypeStruct((RB, CB), F32),
        in_specs=[pl.BlockSpec(memory_space=pltpu.VMEM)] * 2,
        out_specs=pl.BlockSpec(memory_space=pltpu.VMEM),
        scratch_shapes=[
            vmem((RB, NB)),
            vmem((CB, NB)),
            vmem((RB, CB), BF16),
            vmem((RB, CB), BF16),
            vmem((CB, NB), BF16),
            vmem((CB, NB), BF16),
            vmem((RB, NB)),
            vmem((RB // 2, NB)),
            vmem((RB // 2, NB)),
            vmem((NZ, SL, NB)),
            vmem((RB, NB)),
            vmem((CB, NB)),
            vmem((NB, NB)),
            vmem((NB, NB)),
            vmem((NX * GS, NB)),
            vmem((NY * GS, NB)),
            vmem((NX * GS, NB)),
            vmem((NY * GS, NB)),
            vmem((NB, NB)),
            vmem((NB, NB)),
            vmem((NB, NB)),
            vmem((NB, NB)),
            vmem((RB, 2 * NB), BF16),
            vmem((RB, 2 * NB), BF16),
            vmem((CB, 2 * NB), BF16),
            vmem((CB, 2 * NB), BF16),
            dma(NY),
            dma(2, NG),
            dma(3, NG),
            dma(NY),
            dma(2, NG),
            dma(3, NG),
            dma(2),
            dma(2),
            dma(NZ),
            dma(NZ),
            dma(NZ),
            dma(NZ),
            dma(NX),
            dma(NX),
            dma(NY),
            dma(NY),
            dma(NZ),
            dma(NZ),
            dma(2),
            dma(NX),
            dma(NX),
            dma(NY),
            dma(NY),
            dma(NZ),
            dma(NZ),
            dma(2),
        ],
        compiler_params=pltpu.CompilerParams(
            collective_id=1, has_side_effects=True, vmem_limit_bytes=48 * 2**20
        ),
        name="two_sided_update",
    )(matrix, reflectors)


def solution(mesh):
    in_specs = (P("row", "col"), P("row", None))
    out_specs = P("row", "col")
    return jax.shard_map(
        per_device, mesh=mesh, in_specs=in_specs, out_specs=out_specs, check_vma=False
    )
```

```python
import jax
import jax.numpy as jnp
from jax import lax
from jax.experimental import pallas as pl
from jax.experimental.pallas import tpu as pltpu
from jax.sharding import PartitionSpec as P

MESH = pl.DeviceIdType.MESH
F32 = jnp.float32
BF16 = jnp.bfloat16
NX, NY, NZ = 4, 8, 8
RB, CB, NB = 512, 1024, 256
SL = RB // 16
GS = NB // 16
NG = 2
GR = RB // NG
NH = 2
HB = NB // NH
FAR = (4, 3, 5, 2, 6, 1, 7)


def split(value):
    high = value.astype(BF16)
    return high, (value - high.astype(F32)).astype(BF16)


def dims(left, right):
    return (((left,), (right,)), ((), ()))


def dot_split(left, right, contract):
    (lh, ll), (rh, rl) = left, right
    out = lax.dot_general(lh, rl, contract, preferred_element_type=F32)
    out += lax.dot_general(ll, rh, contract, preferred_element_type=F32)
    out += lax.dot_general(lh, rh, contract, preferred_element_type=F32)
    return out


def dot_full(left, right, contract):
    return lax.dot_general(
        left, right, contract, precision=lax.Precision.HIGHEST, preferred_element_type=F32
    )


NN, NT, TN = dims(1, 0), dims(1, 1), dims(0, 0)


def device(x, y, z, k):
    return (y * NX + x, z * 2 + k)


def kernel(a_hbm, v_hbm, o_ref, *scratch):
    (
        a_ref,
        v_ref,
        vm,
        vcol,
        ah,
        al,
        vch,
        vcl,
        ppart,
        swapb,
        psum,
        rsb,
        prow,
        pcol,
        gloc,
        gram,
        gx,
        gy,
        sloc,
        sswap,
        ssum,
        srs,
        smat,
        sx,
        sy,
        res,
        powr,
        vrh,
        vrl,
        wch,
        wcl,
        load_sem,
        v_send,
        v_recv,
        vf_send,
        p_send,
        p_recv,
        pf_send,
        sw_send,
        sw_recv,
        rs_send,
        rs_recv,
        pr_send,
        pr_recv,
        gx_send,
        gx_recv,
        gy_send,
        gy_recv,
        gz_send,
        gz_recv,
        sr_send,
        sr_recv,
        sx_send,
        sx_recv,
        sy_send,
        sy_recv,
        sz_send,
        sz_recv,
    ) = scratch
    grow = lax.axis_index("row")
    gcol = lax.axis_index("col")
    x, y, z, k = grow % NX, grow // NX, gcol // 2, gcol % 2
    kx = x // 2
    hub = k == kx
    mine = 8 * k + z
    twin = device(x, y, z, 1 - k)
    has_self = jnp.logical_and(z == y, hub)
    sent = []

    load_v = pltpu.make_async_copy(v_hbm, v_ref, load_sem.at[0])
    load_v.start()
    load_a = pltpu.make_async_copy(a_hbm, a_ref, load_sem.at[1])
    load_a.start()

    def remote(src, dst, send, recv, target):
        return pltpu.make_async_remote_copy(
            src_ref=src,
            dst_ref=dst,
            send_sem=send,
            recv_sem=recv,
            device_id=target,
            device_id_type=MESH,
        )

    def begin(cp):
        cp.start()
        sent.append(cp)

    def await_part(part, sem):
        pltpu.make_async_copy(part, part, sem).wait()

    x_line = lambda d: device((x + d) % NX, y, z, k)
    y_line = lambda d: device(x, (y + d) % NY, z, k)
    z_line = lambda d: device(x, y, (z + d) % NZ, k)

    barrier = pltpu.get_barrier_semaphore()

    def greet(target):
        pl.semaphore_signal(barrier, inc=1, device_id=target, device_id_type=MESH)

    @pl.when(hub)
    def _():
        for d in (4, 3, 5, 2, 6, 1, 7, 0):
            for e in range(2):
                zz = (z + d) % NZ
                if d == 0:

                    @pl.when(jnp.logical_not(jnp.logical_and(y == z, k == e)))
                    def _():
                        greet(device(x, z, zz, e))
                else:
                    greet(device(x, z, zz, e))

    for d in range(1, NY):
        greet(y_line(d))
    for d in range(1, NZ):
        greet(z_line(d))
    for d in range(1, NX):
        greet(x_line(d))
    greet(twin)

    def masked(value, first, left=0):
        rows = first + lax.broadcasted_iota(jnp.int32, value.shape, 0)
        lead = NB + left + lax.broadcasted_iota(jnp.int32, value.shape, 1)
        return jnp.where(rows > lead, value, jnp.where(rows == lead, 1.0, 0.0).astype(F32))

    load_v.wait()
    vm[...] = masked(v_ref[...], grow * RB)
    gloc[...] = dot_full(vm[...], vm[...], TN)
    gx[pl.ds(x * GS, GS)] = gloc[pl.ds(mine * GS, GS)]

    others = 3 + 7 + 7 + 1 + 8
    pl.semaphore_wait(barrier, others - jnp.where(has_self, 1, 0))

    def spread(src, dst, send, recv, h, start):
        for d in FAR + (0,):
            place = dst.at[h, pl.ds(RB * (x % 2) + SL * mine, SL)]
            sem = recv.at[h, x % 2, k]
            cp = remote(src, place, send.at[h, d], sem, device(x, (y + d) % NY, y, kx))
            if d == 0:

                @pl.when(has_self)
                def _():
                    if start:
                        pltpu.make_async_copy(src, place, sem).start()

                @pl.when(jnp.logical_not(has_self))
                def _():
                    if start:
                        cp.start()
                    else:
                        cp.wait_send()
            elif start:
                cp.start()
            else:
                cp.wait_send()

    def group(ref, h, j, g):
        return ref.at[h, pl.ds(RB * j + GR * g, GR)]

    def place_in_ring(j):
        return (x - 2 * k - j) % NX

    def hub_step(ref, send, recv, h, start=True):
        @pl.when(hub)
        def _():
            for g in range(NG):
                part = group(ref, h, x % 2, g)
                sem = recv.at[h, x % 2, g]
                if start:
                    await_part(part, sem)
                for i, d in enumerate((1, 3) if g == 0 else (3, 1)):
                    cp = remote(part, part, send.at[h, g, i], sem, x_line(d))
                    if start:
                        cp.start()
                    else:
                        cp.wait_send()

    def relay_step(ref, send, recv, h, start=True):
        for g, d in ((0, 1), (1, 3)):
            for j in range(2):

                @pl.when(place_in_ring(j) == d)
                def _():
                    part = group(ref, h, j, g)
                    sem = recv.at[h, j, g]
                    if start:
                        await_part(part, sem)
                    cp = remote(part, part, send.at[h, g, 2], sem, x_line(d))
                    if start:
                        cp.start()
                    else:
                        cp.wait_send()

    def await_group(ref, recv, h, j, g):
        here = place_in_ring(j)

        @pl.when(jnp.logical_and(here != 0, here != (1, 3)[g]))
        def _():
            await_part(group(ref, h, j, g), recv.at[h, j, g])

    def finish(ref, send, recv):
        for h in range(NH):
            hub_step(ref, send, recv, h, False)
            relay_step(ref, send, recv, h, False)

    def lined(buf, own, send, recv, count, make):
        part = buf.at[pl.ds(own * GS, GS)]
        for d in FAR if count == 8 else (2, 1, 3):
            begin(remote(part, part, send.at[d], recv.at[own], make(d)))

    def fold_line(buf, own, recv, count):
        for d in range(1, count):
            other = (own + d) % count
            await_part(buf.at[pl.ds(other * GS, GS)], recv.at[other])
        total = buf[pl.ds(0, GS)]
        for i in range(1, count):
            total = total + buf[pl.ds(i * GS, GS)]
        return total

    def to_z(buf, size, send, recv):
        part = buf.at[pl.ds(mine * size, size)]
        for d in FAR:
            begin(remote(part, part, send.at[d], recv.at[z], z_line(d)))

    def await_z(buf, size, recv):
        for d in range(1, NZ):
            other = (z + d) % NZ
            await_part(buf.at[pl.ds((8 * k + other) * size, size)], recv.at[other])

    def to_twin(buf, size, i):
        part = buf.at[pl.ds(k * size, size)]
        begin(remote(part, part, sw_send.at[i], sw_recv.at[i], twin))

    def await_twin(buf, size, i):
        await_part(buf.at[pl.ds((1 - k) * size, size)], sw_recv.at[i])

    def chunk(h):
        return slice(HB * h, HB * h + HB)

    def v_slice(h):
        return v_ref.at[pl.ds(SL * mine, SL), chunk(h)]

    v_ring = (vcol, vf_send, v_recv)
    p_ring = (pcol, pf_send, p_recv)
    spread(v_slice(0), vcol, v_send, v_recv, 0, True)
    lined(gx, x, gx_send, gx_recv, NX, x_line)
    spread(v_slice(1), vcol, v_send, v_recv, 1, True)

    load_a.wait()

    def split_a(i, carry):
        rows = pl.ds(pl.multiple_of(i * 64, 64), 64)
        high, low = split(a_ref[rows])
        ah[rows] = high
        al[rows] = low
        return carry

    lax.fori_loop(0, RB // 64, split_a, 0)

    gy[pl.ds(y * GS, GS)] = fold_line(gx, x, gx_recv, NX)
    lined(gy, y, gy_send, gy_recv, NY, y_line)
    hub_step(*v_ring, 0)
    hub_step(*v_ring, 1)
    relay_step(*v_ring, 0)
    relay_step(*v_ring, 1)
    gram[pl.ds(mine * GS, GS)] = fold_line(gy, y, gy_recv, NY)
    to_z(gram, GS, gz_send, gz_recv)

    half = RB // 2

    def part_p(h, side):
        rows = pl.ds(pl.multiple_of(side * half, half), half)
        cols = chunk(h)
        ppart[h, rows] = dot_split(
            (ah[rows], al[rows]), (vch[:, cols], vcl[:, cols]), NN
        )

    def begin_p(h):
        for j in range(2):
            for g in range(NG):
                await_group(vcol, v_recv, h, j, g)
            rows = pl.ds(RB * j, RB)
            high, low = split(masked(vcol[h, rows], gcol * CB + RB * j, HB * h))
            vch[rows, chunk(h)] = high
            vcl[rows, chunk(h)] = low
        part_p(h, 1 - k)
        part = ppart.at[h, pl.ds((1 - k) * half, half)]
        begin(remote(part, swapb.at[h], sw_send.at[h], sw_recv.at[h], twin))
        part_p(h, k)

    def sum_p(h):
        await_part(swapb.at[h], sw_recv.at[h])
        psum[h] = ppart[h, pl.ds(k * half, half)] + swapb[h]
        for d in FAR:
            src = psum.at[h, pl.ds((z + d) % NZ * SL, SL)]
            begin(remote(src, rsb.at[h, z], rs_send.at[h, d], rs_recv.at[h, z], z_line(d)))

    own_rows = pl.ds(mine * SL, SL)

    def send_p(h):
        total = psum[h, pl.ds(z * SL, SL)]
        for d in (1, 7, 2, 6, 3, 5, 4):
            other = (z + d) % NZ
            await_part(rsb.at[h, other], rs_recv.at[h, other])
            total = total + rsb[h, other]
        prow[h, own_rows] = total
        spread(prow.at[h, own_rows], pcol, p_send, p_recv, h, True)

    def send_row(h):
        part = prow.at[h, own_rows]
        for d in FAR:
            begin(remote(part, part, pr_send.at[h, d], pr_recv.at[h, z], z_line(d)))

    begin_p(0)
    sum_p(0)
    begin_p(1)
    vsplit = split(vm[...])
    for h in range(NH):
        sloc[:, chunk(h)] = dot_split(vsplit, split(ppart[h]), TN)
    begin(remote(sloc.at[pl.ds((1 - k) * 128, 128)], sswap, sw_send.at[2], sw_recv.at[2], twin))
    sum_p(1)
    await_part(sswap, sw_recv.at[2])
    ssum[...] = sloc[pl.ds(k * 128, 128)] + sswap[...]
    for d in FAR:
        src = ssum.at[pl.ds((z + d) % NZ * GS, GS)]
        begin(remote(src, srs.at[z], sr_send.at[d], sr_recv.at[z], z_line(d)))
    await_z(gram, GS, gz_recv)
    to_twin(gram, 128, 3)

    send_p(0)

    await_twin(gram, 128, 3)
    ri = lax.broadcasted_iota(jnp.int32, (NB, NB), 0)
    ci = lax.broadcasted_iota(jnp.int32, (NB, NB), 1)
    ident = jnp.where(ri == ci, 1.0, 0.0).astype(F32)
    full = gram[...]
    diag = jnp.where(ri == ci, full, 0.0) * 0.5
    inv_col = 1.0 / jnp.sum(diag, axis=1, keepdims=True)
    inv_row = 1.0 / jnp.sum(diag, axis=0, keepdims=True)
    strict = jnp.where(ri < ci, full, 0.0) * inv_col
    res[...] = ident - strict
    powr[...] = dot_full(strict, strict, NN)

    def grow_inverse(i, carry):
        power = powr[...]
        res[...] += dot_full(res[...], power, NN)
        powr[...] = dot_full(power, power, NN)
        return carry

    lax.fori_loop(0, 3, grow_inverse, 0)

    send_p(1)
    for d in FAR:
        other = (z + d) % NZ
        await_part(srs.at[other], sr_recv.at[other])
    total = ssum[pl.ds(z * GS, GS)]
    for d in range(1, NZ):
        total = total + srs[(z + d) % NZ]
    sx[pl.ds(x * GS, GS)] = total
    lined(sx, x, sx_send, sx_recv, NX, x_line)
    send_row(0)
    send_row(1)

    lax.fori_loop(0, 3, grow_inverse, 0)
    hub_step(*p_ring, 0)
    sy[pl.ds(y * GS, GS)] = fold_line(sx, x, sx_recv, NX)
    lined(sy, y, sy_send, sy_recv, NY, y_line)

    res[...] += dot_full(res[...], powr[...], NN)
    tfac = split(res[...] * inv_row)
    high, low = split(dot_split(vsplit, tfac, NT))
    vrh[...] = high
    vrl[...] = low
    hub_step(*p_ring, 1)
    relay_step(*p_ring, 0)

    def wide_cols(i, carry):
        rows = pl.ds(pl.multiple_of(i * 256, 256), 256)
        high, low = split(dot_split((vch[rows], vcl[rows]), tfac, NT))
        wch[rows] = high
        wcl[rows] = low
        return carry

    lax.fori_loop(0, CB // 256, wide_cols, 0)

    smat[pl.ds(mine * GS, GS)] = fold_line(sy, y, sy_recv, NY)
    to_z(smat, GS, sz_send, sz_recv)
    relay_step(*p_ring, 1)
    for h in range(NH):
        for d in FAR:
            other = (z + d) % NZ
            part = prow.at[h, pl.ds((8 * k + other) * SL, SL)]
            await_part(part, pr_recv.at[h, other])
    part = prow.at[:, pl.ds(k * half, half)]
    begin(remote(part, part, sw_send.at[4], sw_recv.at[4], twin))

    def update(from_ref, left, right, rows):
        cols = dot_split(left, right, NT)
        o_ref[:, rows] = from_ref[:, rows] - cols

    def first_part(h, j, g):
        await_group(pcol, p_recv, h, j, g)
        rows = pl.ds(RB * j + GR * g, GR)
        left = (vrh[:, chunk(h)], vrl[:, chunk(h)])
        update(o_ref if h else a_ref, left, split(pcol[h, rows]), rows)

    for g in range(NG):
        for j in range(2):
            first_part(0, j, g)

    await_z(smat, GS, sz_recv)
    to_twin(smat, 128, 5)
    for g in range(NG):
        for j in range(2):
            first_part(1, j, g)

    await_part(prow.at[:, pl.ds((1 - k) * half, half)], sw_recv.at[4])
    await_twin(smat, 128, 5)
    inner = dot_split((vrh[...], vrl[...]), split(smat[...]), NN)
    parts = [split(prow[h] - inner[:, chunk(h)]) for h in range(NH)]
    rest = tuple(jnp.concatenate([part[i] for part in parts], axis=1) for i in range(2))
    for i in range(CB // 256):
        rows = pl.ds(256 * i, 256)
        update(o_ref, rest, (wch[rows], wcl[rows]), rows)

    for h in range(NH):
        spread(v_slice(h), vcol, v_send, v_recv, h, False)
        spread(prow.at[h, own_rows], pcol, p_send, p_recv, h, False)
    finish(*v_ring)
    finish(*p_ring)
    for cp in sent:
        cp.wait_send()


def per_device(matrix, reflectors):
    vmem = lambda shape, kind=F32: pltpu.VMEM(shape, kind)
    dma = lambda *shape: pltpu.SemaphoreType.DMA(shape)
    return pl.pallas_call(
        kernel,
        out_shape=pltpu.VMEM((RB, CB), F32),
        in_specs=[pl.BlockSpec(memory_space=pltpu.HBM)] * 2,
        out_specs=pl.BlockSpec(memory_space=pltpu.VMEM),
        scratch_shapes=[
            vmem((RB, CB)),
            vmem((RB, NB)),
            vmem((RB, NB)),
            vmem((NH, CB, HB)),
            vmem((RB, CB), BF16),
            vmem((RB, CB), BF16),
            vmem((CB, NB), BF16),
            vmem((CB, NB), BF16),
            vmem((NH, RB, HB)),
            vmem((NH, RB // 2, HB)),
            vmem((NH, RB // 2, HB)),
            vmem((NH, NZ, SL, HB)),
            vmem((NH, RB, HB)),
            vmem((NH, CB, HB)),
            vmem((NB, NB)),
            vmem((NB, NB)),
            vmem((NX * GS, NB)),
            vmem((NY * GS, NB)),
            vmem((NB, NB)),
            vmem((NB // 2, NB)),
            vmem((NB // 2, NB)),
            vmem((NZ, GS, NB)),
            vmem((NB, NB)),
            vmem((NX * GS, NB)),
            vmem((NY * GS, NB)),
            vmem((NB, NB)),
            vmem((NB, NB)),
            vmem((RB, NB), BF16),
            vmem((RB, NB), BF16),
            vmem((CB, NB), BF16),
            vmem((CB, NB), BF16),
            dma(2),
            dma(NH, NY),
            dma(NH, 2, NG),
            dma(NH, NG, 3),
            dma(NH, NY),
            dma(NH, 2, NG),
            dma(NH, NG, 3),
            dma(6),
            dma(6),
            dma(NH, NZ),
            dma(NH, NZ),
            dma(NH, NZ),
            dma(NH, NZ),
            dma(NX),
            dma(NX),
            dma(NY),
            dma(NY),
            dma(NZ),
            dma(NZ),
            dma(NZ),
            dma(NZ),
            dma(NX),
            dma(NX),
            dma(NY),
            dma(NY),
            dma(NZ),
            dma(NZ),
        ],
        compiler_params=pltpu.CompilerParams(
            collective_id=1, has_side_effects=True, vmem_limit_bytes=60 * 2**20
        ),
        name="two_sided_update",
    )(matrix, reflectors)


def solution(mesh):
    in_specs = (P("row", "col"), P("row", None))
    out_specs = P("row", "col")
    return jax.shard_map(
        per_device, mesh=mesh, in_specs=in_specs, out_specs=out_specs, check_vma=False
    )
```

```python
import jax
import jax.numpy as jnp
from jax import lax
from jax.experimental import pallas as pl
from jax.experimental.pallas import tpu as pltpu
from jax.sharding import PartitionSpec as P

MESH = pl.DeviceIdType.MESH
F32 = jnp.float32
BF16 = jnp.bfloat16
NX, NY, NZ = 4, 8, 8
RB, CB, NB = 512, 1024, 256
SL = RB // 16
GS = NB // 16
NG = 4
GR = RB // NG
NH = 2
HB = NB // NH
FAR = (4, 3, 5, 2, 6, 1, 7)


def split(value):
    high = value.astype(BF16)
    return high, (value - high.astype(F32)).astype(BF16)


def dims(left, right):
    return (((left,), (right,)), ((), ()))


def dot_split(left, right, contract):
    (lh, ll), (rh, rl) = left, right
    out = lax.dot_general(lh, rl, contract, preferred_element_type=F32)
    out += lax.dot_general(ll, rh, contract, preferred_element_type=F32)
    out += lax.dot_general(lh, rh, contract, preferred_element_type=F32)
    return out


def dot_full(left, right, contract):
    return lax.dot_general(
        left, right, contract, precision=lax.Precision.HIGHEST, preferred_element_type=F32
    )


NN, NT, TN = dims(1, 0), dims(1, 1), dims(0, 0)


def device(x, y, z, k):
    return (y * NX + x, z * 2 + k)


def kernel(a_hbm, v_hbm, o_ref, *scratch):
    (
        a_ref,
        v_ref,
        vm,
        vcol,
        ah,
        al,
        vch,
        vcl,
        ppart,
        swapb,
        psum,
        rsb,
        prow,
        pcol,
        gloc,
        gram,
        gx,
        gy,
        sloc,
        sswap,
        ssum,
        srs,
        smat,
        sx,
        sy,
        res,
        vrh,
        vrl,
        wch,
        wcl,
        wth,
        wtl,
        load_sem,
        v_send,
        v_recv,
        vf_send,
        p_send,
        p_recv,
        pf_send,
        sw_send,
        sw_recv,
        rs_send,
        rs_recv,
        pr_send,
        pr_recv,
        gx_send,
        gx_recv,
        gy_send,
        gy_recv,
        gz_send,
        gz_recv,
        sr_send,
        sr_recv,
        sx_send,
        sx_recv,
        sy_send,
        sy_recv,
        sz_send,
        sz_recv,
    ) = scratch
    grow = lax.axis_index("row")
    gcol = lax.axis_index("col")
    x, y, z, k = grow % NX, grow // NX, gcol // 2, gcol % 2
    kx = x // 2
    hub = k == kx
    mine = 8 * k + z
    twin = device(x, y, z, 1 - k)
    has_self = jnp.logical_and(z == y, hub)
    sent = []

    load_v = pltpu.make_async_copy(v_hbm, v_ref, load_sem.at[0])
    load_v.start()
    load_a = pltpu.make_async_copy(a_hbm, a_ref, load_sem.at[1])
    load_a.start()

    def remote(src, dst, send, recv, target):
        return pltpu.make_async_remote_copy(
            src_ref=src,
            dst_ref=dst,
            send_sem=send,
            recv_sem=recv,
            device_id=target,
            device_id_type=MESH,
        )

    def begin(cp):
        cp.start()
        sent.append(cp)

    def await_part(part, sem):
        pltpu.make_async_copy(part, part, sem).wait()

    x_line = lambda d: device((x + d) % NX, y, z, k)
    y_line = lambda d: device(x, (y + d) % NY, z, k)
    z_line = lambda d: device(x, y, (z + d) % NZ, k)

    barrier = pltpu.get_barrier_semaphore()

    def greet(target):
        pl.semaphore_signal(barrier, inc=1, device_id=target, device_id_type=MESH)

    @pl.when(hub)
    def _():
        for d in (4, 3, 5, 2, 6, 1, 7, 0):
            for e in range(2):
                zz = (z + d) % NZ
                if d == 0:

                    @pl.when(jnp.logical_not(jnp.logical_and(y == z, k == e)))
                    def _():
                        greet(device(x, z, zz, e))
                else:
                    greet(device(x, z, zz, e))

    for d in range(1, NY):
        greet(y_line(d))
    for d in range(1, NZ):
        greet(z_line(d))
    for d in range(1, NX):
        greet(x_line(d))
    greet(twin)

    def masked(value, first, left=0):
        rows = first + lax.broadcasted_iota(jnp.int32, value.shape, 0)
        lead = NB + left + lax.broadcasted_iota(jnp.int32, value.shape, 1)
        return jnp.where(rows > lead, value, jnp.where(rows == lead, 1.0, 0.0).astype(F32))

    load_v.wait()
    vm[...] = masked(v_ref[...], grow * RB)
    gloc[...] = dot_full(vm[...], vm[...], TN)
    gx[pl.ds(x * GS, GS)] = gloc[pl.ds(mine * GS, GS)]

    others = 3 + 7 + 7 + 1 + 8
    pl.semaphore_wait(barrier, others - jnp.where(has_self, 1, 0))

    def spread(src, dst, send, recv, h, start):
        for d in FAR + (0,):
            place = dst.at[h, pl.ds(RB * (x % 2) + SL * mine, SL)]
            sem = recv.at[h, x % 2, mine // (16 // NG)]
            cp = remote(src, place, send.at[h, d], sem, device(x, (y + d) % NY, y, kx))
            if d == 0:

                @pl.when(has_self)
                def _():
                    if start:
                        pltpu.make_async_copy(src, place, sem).start()

                @pl.when(jnp.logical_not(has_self))
                def _():
                    if start:
                        cp.start()
                    else:
                        cp.wait_send()
            elif start:
                cp.start()
            else:
                cp.wait_send()

    def group(ref, h, j, g):
        return ref.at[h, pl.ds(RB * j + GR * g, GR)]

    def hub_step(ref, send, recv, h, start=True):
        @pl.when(hub)
        def _():
            near = z // 4
            for i in range(NG):
                g = (near if i < 2 else 1 - near) + 2 * (i % 2)
                part = group(ref, h, x % 2, g)
                sem = recv.at[h, x % 2, g]
                if start:
                    await_part(part, sem)
                for d in (2, 1, 3):
                    cp = remote(part, part, send.at[h, i, d - 1], sem, x_line(d))
                    if start:
                        cp.start()
                    else:
                        cp.wait_send()

    def await_group(ref, recv, h, j, g):
        @pl.when(jnp.logical_not(jnp.logical_and(hub, x % 2 == j)))
        def _():
            await_part(group(ref, h, j, g), recv.at[h, j, g])

    def finish(ref, send, recv):
        for h in range(NH):
            hub_step(ref, send, recv, h, False)

    def lined(buf, own, send, recv, count, make):
        part = buf.at[pl.ds(own * GS, GS)]
        for d in FAR if count == 8 else (2, 1, 3):
            begin(remote(part, part, send.at[d], recv.at[own], make(d)))

    def fold_line(buf, own, recv, count):
        for d in range(1, count):
            other = (own + d) % count
            await_part(buf.at[pl.ds(other * GS, GS)], recv.at[other])
        total = buf[pl.ds(0, GS)]
        for i in range(1, count):
            total = total + buf[pl.ds(i * GS, GS)]
        return total

    def to_z(buf, size, send, recv):
        part = buf.at[pl.ds(mine * size, size)]
        for d in FAR:
            begin(remote(part, part, send.at[d], recv.at[z], z_line(d)))

    def await_z(buf, size, recv):
        for d in range(1, NZ):
            other = (z + d) % NZ
            await_part(buf.at[pl.ds((8 * k + other) * size, size)], recv.at[other])

    def to_twin(buf, size, i):
        part = buf.at[pl.ds(k * size, size)]
        begin(remote(part, part, sw_send.at[i], sw_recv.at[i], twin))

    def await_twin(buf, size, i):
        await_part(buf.at[pl.ds((1 - k) * size, size)], sw_recv.at[i])

    def chunk(h):
        return slice(HB * h, HB * h + HB)

    def v_slice(h):
        return v_ref.at[pl.ds(SL * mine, SL), chunk(h)]

    v_ring = (vcol, vf_send, v_recv)
    p_ring = (pcol, pf_send, p_recv)
    spread(v_slice(0), vcol, v_send, v_recv, 0, True)
    lined(gx, x, gx_send, gx_recv, NX, x_line)
    spread(v_slice(1), vcol, v_send, v_recv, 1, True)

    load_a.wait()

    def split_a(i, carry):
        rows = pl.ds(pl.multiple_of(i * 64, 64), 64)
        high, low = split(a_ref[rows])
        ah[rows] = high
        al[rows] = low
        return carry

    lax.fori_loop(0, RB // 64, split_a, 0)

    def part_w(i, carry):
        rows = pl.ds(pl.multiple_of(i * 256, 256), 256)
        high, low = split(dot_split((ah[:, rows], al[:, rows]), split(vm[...]), TN))
        wth[rows] = high
        wtl[rows] = low
        return carry

    lax.fori_loop(0, CB // 256, part_w, 0)

    gy[pl.ds(y * GS, GS)] = fold_line(gx, x, gx_recv, NX)
    lined(gy, y, gy_send, gy_recv, NY, y_line)
    hub_step(*v_ring, 0)
    hub_step(*v_ring, 1)
    gram[pl.ds(mine * GS, GS)] = fold_line(gy, y, gy_recv, NY)
    to_z(gram, GS, gz_send, gz_recv)

    half = RB // 2

    def part_p(h, side):
        rows = pl.ds(pl.multiple_of(side * half, half), half)
        cols = chunk(h)
        ppart[h, rows] = dot_split(
            (ah[rows], al[rows]), (vch[:, cols], vcl[:, cols]), NN
        )

    def begin_p(h):
        for j in range(2):
            for g in range(NG):
                await_group(vcol, v_recv, h, j, g)
            rows = pl.ds(RB * j, RB)
            high, low = split(masked(vcol[h, rows], gcol * CB + RB * j, HB * h))
            vch[rows, chunk(h)] = high
            vcl[rows, chunk(h)] = low
        part_p(h, 1 - k)
        part = ppart.at[h, pl.ds((1 - k) * half, half)]
        begin(remote(part, swapb.at[h], sw_send.at[h], sw_recv.at[h], twin))
        cols = chunk(h)
        sloc[cols] = dot_split((vch[:, cols], vcl[:, cols]), (wth[...], wtl[...]), TN)

        @pl.when(k != h)
        def _():
            s_swap.start()

        part_p(h, k)

    def sum_p(h):
        await_part(swapb.at[h], sw_recv.at[h])
        psum[h] = ppart[h, pl.ds(k * half, half)] + swapb[h]
        for d in FAR:
            src = psum.at[h, pl.ds((z + d) % NZ * SL, SL)]
            begin(remote(src, rsb.at[h, z], rs_send.at[h, d], rs_recv.at[h, z], z_line(d)))

    own_rows = pl.ds(mine * SL, SL)

    def line_copies(buf, own, send, recv, order, make):
        part = buf.at[pl.ds(own * GS, GS)]
        return [remote(part, part, send.at[d], recv.at[own], make(d)) for d in order]

    own_s = smat.at[pl.ds(mine * GS, GS)]
    half_s = smat.at[pl.ds(k * 128, 128)]
    s_swap = remote(sloc.at[pl.ds((1 - k) * 128, 128)], sswap, sw_send.at[2], sw_recv.at[2], twin)
    s_rs = [
        remote(
            ssum.at[pl.ds((z + d) % NZ * GS, GS)], srs.at[z], sr_send.at[d], sr_recv.at[z], z_line(d)
        )
        for d in FAR
    ]
    s_xs = line_copies(sx, x, sx_send, sx_recv, (2, 1, 3), x_line)
    s_ys = line_copies(sy, y, sy_send, sy_recv, FAR, y_line)
    s_zs = [remote(own_s, own_s, sz_send.at[d], sz_recv.at[z], z_line(d)) for d in FAR]
    s_share = remote(half_s, half_s, sw_send.at[5], sw_recv.at[5], twin)
    sent.extend([s_swap, s_share] + s_rs + s_xs + s_ys + s_zs)

    def send_p(h):
        total = psum[h, pl.ds(z * SL, SL)]
        for d in (1, 7, 2, 6, 3, 5, 4):
            other = (z + d) % NZ
            await_part(rsb.at[h, other], rs_recv.at[h, other])
            total = total + rsb[h, other]
        prow[h, own_rows] = total
        spread(prow.at[h, own_rows], pcol, p_send, p_recv, h, True)

    def send_row(h):
        part = prow.at[h, own_rows]
        for d in FAR:
            begin(remote(part, part, pr_send.at[h, d], pr_recv.at[h, z], z_line(d)))

    def s_sum():
        await_part(sswap, sw_recv.at[2])
        ssum[...] = sloc[pl.ds(k * 128, 128)] + sswap[...]
        for cp in s_rs:
            cp.start()

    def s_x():
        for d in FAR:
            other = (z + d) % NZ
            await_part(srs.at[other], sr_recv.at[other])
        total = ssum[pl.ds(z * GS, GS)]
        for d in range(1, NZ):
            total = total + srs[(z + d) % NZ]
        sx[pl.ds(x * GS, GS)] = total
        for cp in s_xs:
            cp.start()

    def s_y():
        sy[pl.ds(y * GS, GS)] = fold_line(sx, x, sx_recv, NX)
        for cp in s_ys:
            cp.start()

    def s_z():
        smat[pl.ds(mine * GS, GS)] = fold_line(sy, y, sy_recv, NY)
        for cp in s_zs:
            cp.start()

    def s_twin():
        await_z(smat, GS, sz_recv)
        s_share.start()

    def on_core(core, step):
        @pl.when(k == core)
        def _():
            step()

    begin_p(0)
    sum_p(0)
    on_core(0, s_sum)
    begin_p(1)
    sum_p(1)
    on_core(1, s_sum)
    await_z(gram, GS, gz_recv)
    to_twin(gram, 128, 3)

    send_p(0)
    on_core(0, s_x)

    await_twin(gram, 128, 3)
    ri = lax.broadcasted_iota(jnp.int32, (NB, NB), 0)
    ci = lax.broadcasted_iota(jnp.int32, (NB, NB), 1)
    ident = jnp.where(ri == ci, 1.0, 0.0).astype(F32)
    full = gram[...]
    diag = jnp.where(ri == ci, full, 0.0) * 0.5
    inv_col = 1.0 / jnp.sum(diag, axis=1, keepdims=True)
    inv_row = 1.0 / jnp.sum(diag, axis=0, keepdims=True)
    strict = jnp.where(ri < ci, full, 0.0) * inv_col
    mid = NB // 2
    eye = ident[:mid, :mid]
    blocks = []
    for b in (slice(0, mid), slice(mid, NB)):
        blocks.append([eye - strict[b, b], dot_full(strict[b, b], strict[b, b], NN)])
    span = 2
    while span < mid:
        for pair in blocks:
            result, power = pair
            pair[0] = result + dot_full(result, power, NN)
            if 2 * span < mid:
                pair[1] = dot_full(power, power, NN)
        span = span * 2
    first, second = blocks[0][0], blocks[1][0]
    corner = -dot_full(dot_full(first, strict[:mid, mid:], NN), second, NN)
    res[:mid] = jnp.concatenate([first, corner], axis=1) * inv_row
    res[mid:] = jnp.concatenate([jnp.zeros((mid, mid), F32), second], axis=1) * inv_row

    on_core(0, s_y)
    send_p(1)
    on_core(1, s_x)
    send_row(0)
    send_row(1)

    tfac = split(res[...])
    high, low = split(dot_split(split(vm[...]), tfac, NT))
    vrh[...] = high
    vrl[...] = low

    def wide_cols(i, carry):
        rows = pl.ds(pl.multiple_of(i * 256, 256), 256)
        high, low = split(dot_split((vch[rows], vcl[rows]), tfac, NT))
        wch[rows] = high
        wcl[rows] = low
        return carry

    lax.fori_loop(0, CB // 256, wide_cols, 0)

    hub_step(*p_ring, 0)
    on_core(1, s_y)
    on_core(0, s_z)
    hub_step(*p_ring, 1)
    on_core(1, s_z)
    for h in range(NH):
        for d in FAR:
            other = (z + d) % NZ
            part = prow.at[h, pl.ds((8 * k + other) * SL, SL)]
            await_part(part, pr_recv.at[h, other])
    part = prow.at[:, pl.ds(k * half, half)]
    begin(remote(part, part, sw_send.at[4], sw_recv.at[4], twin))

    on_core(0, s_twin)

    def update(from_ref, left, right, rows):
        cols = dot_split(left, right, NT)
        o_ref[:, rows] = from_ref[:, rows] - cols

    def first_part(h, j, q):
        for g in range(q * NG // 2, (q + 1) * NG // 2):
            await_group(pcol, p_recv, h, j, g)
        rows = pl.ds(RB * j + 256 * q, 256)
        left = (vrh[:, chunk(h)], vrl[:, chunk(h)])
        update(o_ref if h else a_ref, left, split(pcol[h, rows]), rows)

    for q in range(2):
        for j in range(2):
            first_part(0, j, q)

    on_core(1, s_twin)
    for q in range(2):
        for j in range(2):
            first_part(1, j, q)

    await_part(prow.at[:, pl.ds((1 - k) * half, half)], sw_recv.at[4])
    await_twin(smat, 128, 5)
    inner = dot_split((vrh[...], vrl[...]), split(smat[...]), NN)
    parts = [split(prow[h] - inner[:, chunk(h)]) for h in range(NH)]
    rest = tuple(jnp.concatenate([part[i] for part in parts], axis=1) for i in range(2))
    for i in range(CB // 256):
        rows = pl.ds(256 * i, 256)
        update(o_ref, rest, (wch[rows], wcl[rows]), rows)

    for h in range(NH):
        spread(v_slice(h), vcol, v_send, v_recv, h, False)
        spread(prow.at[h, own_rows], pcol, p_send, p_recv, h, False)
    finish(*v_ring)
    finish(*p_ring)
    for cp in sent:
        cp.wait_send()


def per_device(matrix, reflectors):
    vmem = lambda shape, kind=F32: pltpu.VMEM(shape, kind)
    dma = lambda *shape: pltpu.SemaphoreType.DMA(shape)
    return pl.pallas_call(
        kernel,
        out_shape=pltpu.VMEM((RB, CB), F32),
        in_specs=[pl.BlockSpec(memory_space=pltpu.HBM)] * 2,
        out_specs=pl.BlockSpec(memory_space=pltpu.VMEM),
        scratch_shapes=[
            vmem((RB, CB)),
            vmem((RB, NB)),
            vmem((RB, NB)),
            vmem((NH, CB, HB)),
            vmem((RB, CB), BF16),
            vmem((RB, CB), BF16),
            vmem((CB, NB), BF16),
            vmem((CB, NB), BF16),
            vmem((NH, RB, HB)),
            vmem((NH, RB // 2, HB)),
            vmem((NH, RB // 2, HB)),
            vmem((NH, NZ, SL, HB)),
            vmem((NH, RB, HB)),
            vmem((NH, CB, HB)),
            vmem((NB, NB)),
            vmem((NB, NB)),
            vmem((NX * GS, NB)),
            vmem((NY * GS, NB)),
            vmem((NB, NB)),
            vmem((NB // 2, NB)),
            vmem((NB // 2, NB)),
            vmem((NZ, GS, NB)),
            vmem((NB, NB)),
            vmem((NX * GS, NB)),
            vmem((NY * GS, NB)),
            vmem((NB, NB)),
            vmem((RB, NB), BF16),
            vmem((RB, NB), BF16),
            vmem((CB, NB), BF16),
            vmem((CB, NB), BF16),
            vmem((CB, NB), BF16),
            vmem((CB, NB), BF16),
            dma(2),
            dma(NH, NY),
            dma(NH, 2, NG),
            dma(NH, NG, 3),
            dma(NH, NY),
            dma(NH, 2, NG),
            dma(NH, NG, 3),
            dma(6),
            dma(6),
            dma(NH, NZ),
            dma(NH, NZ),
            dma(NH, NZ),
            dma(NH, NZ),
            dma(NX),
            dma(NX),
            dma(NY),
            dma(NY),
            dma(NZ),
            dma(NZ),
            dma(NZ),
            dma(NZ),
            dma(NX),
            dma(NX),
            dma(NY),
            dma(NY),
            dma(NZ),
            dma(NZ),
        ],
        compiler_params=pltpu.CompilerParams(
            collective_id=1, has_side_effects=True, vmem_limit_bytes=60 * 2**20
        ),
        name="two_sided_update",
    )(matrix, reflectors)


def solution(mesh):
    in_specs = (P("row", "col"), P("row", None))
    out_specs = P("row", "col")
    return jax.shard_map(
        per_device, mesh=mesh, in_specs=in_specs, out_specs=out_specs, check_vma=False
    )
```

```python
import jax
import jax.numpy as jnp
from jax import lax
from jax.experimental import pallas as pl
from jax.experimental.pallas import tpu as pltpu
from jax.sharding import PartitionSpec as P

MESH = pl.DeviceIdType.MESH
F32 = jnp.float32
BF16 = jnp.bfloat16
NX, NY, NZ = 4, 8, 8
RB, CB, NB = 512, 1024, 256
SL = RB // 16
GS = NB // 16
NG = 4
GR = RB // NG
NH = 2
HB = NB // NH
FAR = (4, 3, 5, 2, 6, 1, 7)


def split(value):
    high = value.astype(BF16)
    return high, (value - high.astype(F32)).astype(BF16)


def dims(left, right):
    return (((left,), (right,)), ((), ()))


def dot_split(left, right, contract):
    (lh, ll), (rh, rl) = left, right
    out = lax.dot_general(lh, rl, contract, preferred_element_type=F32)
    out += lax.dot_general(ll, rh, contract, preferred_element_type=F32)
    out += lax.dot_general(lh, rh, contract, preferred_element_type=F32)
    return out


def dot_full(left, right, contract):
    return lax.dot_general(
        left, right, contract, precision=lax.Precision.HIGHEST, preferred_element_type=F32
    )


NN, NT, TN = dims(1, 0), dims(1, 1), dims(0, 0)


def device(x, y, z, k):
    return (y * NX + x, z * 2 + k)


def kernel(a_hbm, v_hbm, o_ref, *scratch):
    (
        a_ref,
        v_ref,
        vm,
        vcol,
        ah,
        al,
        vch,
        vcl,
        ppart,
        swapb,
        psum,
        rsb,
        prow,
        pcol,
        gloc,
        gram,
        gx,
        gy,
        sloc,
        sswap,
        ssum,
        srs,
        smat,
        sx,
        sy,
        res,
        vrh,
        vrl,
        wch,
        wcl,
        wth,
        wtl,
        load_sem,
        v_send,
        v_recv,
        vf_send,
        p_send,
        p_recv,
        pf_send,
        sw_send,
        sw_recv,
        rs_send,
        rs_recv,
        pr_send,
        pr_recv,
        gx_send,
        gx_recv,
        gy_send,
        gy_recv,
        gz_send,
        gz_recv,
        sr_send,
        sr_recv,
        sx_send,
        sx_recv,
        sy_send,
        sy_recv,
        sz_send,
        sz_recv,
    ) = scratch
    grow = lax.axis_index("row")
    gcol = lax.axis_index("col")
    x, y, z, k = grow % NX, grow // NX, gcol // 2, gcol % 2
    kx = x // 2
    hub = k == kx
    mine = 8 * k + z
    near = (z - y + NZ + 2) % NZ
    part_of = 8 * k + near
    twin = device(x, y, z, 1 - k)
    has_self = jnp.logical_and(z == y, hub)
    sent = []

    load_v = pltpu.make_async_copy(v_hbm, v_ref, load_sem.at[0])
    load_v.start()
    load_a = pltpu.make_async_copy(a_hbm, a_ref, load_sem.at[1])

    def remote(src, dst, send, recv, target):
        return pltpu.make_async_remote_copy(
            src_ref=src,
            dst_ref=dst,
            send_sem=send,
            recv_sem=recv,
            device_id=target,
            device_id_type=MESH,
        )

    def begin(cp):
        cp.start()
        sent.append(cp)

    def await_part(part, sem):
        pltpu.make_async_copy(part, part, sem).wait()

    x_line = lambda d: device((x + d) % NX, y, z, k)
    y_line = lambda d: device(x, (y + d) % NY, z, k)
    z_line = lambda d: device(x, y, (z + d) % NZ, k)

    barrier = pltpu.get_barrier_semaphore()

    def greet(target):
        pl.semaphore_signal(barrier, inc=1, device_id=target, device_id_type=MESH)

    @pl.when(hub)
    def _():
        for d in (4, 3, 5, 2, 6, 1, 7, 0):
            for e in range(2):
                zz = (z + d) % NZ
                if d == 0:

                    @pl.when(jnp.logical_not(jnp.logical_and(y == z, k == e)))
                    def _():
                        greet(device(x, z, zz, e))
                else:
                    greet(device(x, z, zz, e))

    for d in range(1, NY):
        greet(y_line(d))
    for d in range(1, NZ):
        greet(z_line(d))
    for d in range(1, NX):
        greet(x_line(d))
    greet(twin)

    def masked(value, first, left=0):
        rows = first + lax.broadcasted_iota(jnp.int32, value.shape, 0)
        lead = NB + left + lax.broadcasted_iota(jnp.int32, value.shape, 1)
        return jnp.where(rows > lead, value, jnp.where(rows == lead, 1.0, 0.0).astype(F32))

    others = 3 + 7 + 7 + 1 + 8
    pl.semaphore_wait(barrier, others - jnp.where(has_self, 1, 0))

    def spread(src, dst, send, recv, h, start):
        for d in FAR + (0,):
            place = dst.at[h, pl.ds(RB * (x % 2) + SL * part_of, SL)]
            sem = recv.at[h, x % 2, part_of // (16 // NG)]
            cp = remote(src, place, send.at[h, d], sem, device(x, (y + d) % NY, y, kx))
            if d == 0:

                @pl.when(has_self)
                def _():
                    if start:
                        pltpu.make_async_copy(src, place, sem).start()

                @pl.when(jnp.logical_not(has_self))
                def _():
                    if start:
                        cp.start()
                    else:
                        cp.wait_send()
            elif start:
                cp.start()
            else:
                cp.wait_send()

    def group(ref, h, j, g):
        return ref.at[h, pl.ds(RB * j + GR * g, GR)]

    def hub_step(ref, send, recv, h, start=True):
        @pl.when(hub)
        def _():
            for i in range(NG):
                g = i // 2 + 2 * (i % 2)
                part = group(ref, h, x % 2, g)
                sem = recv.at[h, x % 2, g]
                if start:
                    await_part(part, sem)
                for d in (2, 1, 3):
                    cp = remote(part, part, send.at[h, i, d - 1], sem, x_line(d))
                    if start:
                        cp.start()
                    else:
                        cp.wait_send()

    def await_group(ref, recv, h, j, g):
        @pl.when(jnp.logical_not(jnp.logical_and(hub, x % 2 == j)))
        def _():
            await_part(group(ref, h, j, g), recv.at[h, j, g])

    def finish(ref, send, recv):
        for h in range(NH):
            hub_step(ref, send, recv, h, False)

    def all_left():
        for cp in sent:
            cp.wait_send()
        sent.clear()

    def lined(buf, own, send, recv, count, make):
        part = buf.at[pl.ds(own * GS, GS)]
        for d in FAR if count == 8 else (2, 1, 3):
            begin(remote(part, part, send.at[d], recv.at[own], make(d)))

    def fold_line(buf, own, recv, count):
        for d in range(1, count):
            other = (own + d) % count
            await_part(buf.at[pl.ds(other * GS, GS)], recv.at[other])
        total = buf[pl.ds(0, GS)]
        for i in range(1, count):
            total = total + buf[pl.ds(i * GS, GS)]
        return total

    def to_z(buf, size, send, recv):
        part = buf.at[pl.ds(mine * size, size)]
        for d in FAR:
            begin(remote(part, part, send.at[d], recv.at[z], z_line(d)))

    def await_z(buf, size, recv):
        for d in range(1, NZ):
            other = (z + d) % NZ
            await_part(buf.at[pl.ds((8 * k + other) * size, size)], recv.at[other])

    def to_twin(buf, size, i):
        part = buf.at[pl.ds(k * size, size)]
        begin(remote(part, part, sw_send.at[i], sw_recv.at[i], twin))

    def await_twin(buf, size, i):
        await_part(buf.at[pl.ds((1 - k) * size, size)], sw_recv.at[i])

    def chunk(h):
        return slice(HB * h, HB * h + HB)

    def v_slice(h):
        return v_hbm.at[pl.ds(SL * part_of, SL), chunk(h)]

    v_ring = (vcol, vf_send, v_recv)
    p_ring = (pcol, pf_send, p_recv)
    spread(v_slice(0), vcol, v_send, v_recv, 0, True)
    spread(v_slice(1), vcol, v_send, v_recv, 1, True)
    load_a.start()

    load_v.wait()
    vm[...] = masked(v_ref[...], grow * RB)
    gloc[...] = dot_full(vm[...], vm[...], TN)
    gx[pl.ds(x * GS, GS)] = gloc[pl.ds(mine * GS, GS)]

    lined(gx, x, gx_send, gx_recv, NX, x_line)

    load_a.wait()

    def split_a(i, carry):
        rows = pl.ds(pl.multiple_of(i * 64, 64), 64)
        high, low = split(a_ref[rows])
        ah[rows] = high
        al[rows] = low
        return carry

    lax.fori_loop(0, RB // 64, split_a, 0)

    def part_w(i, carry):
        rows = pl.ds(pl.multiple_of(i * 256, 256), 256)
        high, low = split(dot_split((ah[:, rows], al[:, rows]), split(vm[...]), TN))
        wth[rows] = high
        wtl[rows] = low
        return carry

    lax.fori_loop(0, CB // 256, part_w, 0)

    gy[pl.ds(y * GS, GS)] = fold_line(gx, x, gx_recv, NX)
    lined(gy, y, gy_send, gy_recv, NY, y_line)
    hub_step(*v_ring, 0)
    hub_step(*v_ring, 1)
    gram[pl.ds(mine * GS, GS)] = fold_line(gy, y, gy_recv, NY)
    to_z(gram, GS, gz_send, gz_recv)

    half = RB // 2

    def part_p(h, side):
        rows = pl.ds(pl.multiple_of(side * half, half), half)
        cols = chunk(h)
        ppart[h, rows] = dot_split(
            (ah[rows], al[rows]), (vch[:, cols], vcl[:, cols]), NN
        )

    def begin_p(h):
        for j in range(2):
            for g in range(NG):
                await_group(vcol, v_recv, h, j, g)
            rows = pl.ds(RB * j, RB)
            high, low = split(masked(vcol[h, rows], gcol * CB + RB * j, HB * h))
            vch[rows, chunk(h)] = high
            vcl[rows, chunk(h)] = low
        part_p(h, 1 - k)
        part = ppart.at[h, pl.ds((1 - k) * half, half)]
        begin(remote(part, swapb.at[h], sw_send.at[h], sw_recv.at[h], twin))
        cols = chunk(h)
        sloc[cols] = dot_split((vch[:, cols], vcl[:, cols]), (wth[...], wtl[...]), TN)

        @pl.when(k != h)
        def _():
            s_swap.start()

        part_p(h, k)

    def sum_p(h):
        await_part(swapb.at[h], sw_recv.at[h])
        psum[h] = ppart[h, pl.ds(k * half, half)] + swapb[h]
        for d in FAR:
            src = psum.at[h, pl.ds((near + d) % NZ * SL, SL)]
            begin(remote(src, rsb.at[h, z], rs_send.at[h, d], rs_recv.at[h, z], z_line(d)))

    own_rows = pl.ds(part_of * SL, SL)

    def line_copies(buf, own, send, recv, order, make):
        part = buf.at[pl.ds(own * GS, GS)]
        return [remote(part, part, send.at[d], recv.at[own], make(d)) for d in order]

    own_s = smat.at[pl.ds(mine * GS, GS)]
    half_s = smat.at[pl.ds(k * 128, 128)]
    s_swap = remote(sloc.at[pl.ds((1 - k) * 128, 128)], sswap, sw_send.at[2], sw_recv.at[2], twin)
    s_rs = [
        remote(
            ssum.at[pl.ds((z + d) % NZ * GS, GS)], srs.at[z], sr_send.at[d], sr_recv.at[z], z_line(d)
        )
        for d in FAR
    ]
    s_xs = line_copies(sx, x, sx_send, sx_recv, (2, 1, 3), x_line)
    s_ys = line_copies(sy, y, sy_send, sy_recv, FAR, y_line)
    s_zs = [remote(own_s, own_s, sz_send.at[d], sz_recv.at[z], z_line(d)) for d in FAR]
    s_share = remote(half_s, half_s, sw_send.at[5], sw_recv.at[5], twin)
    sent.extend([s_swap] + s_rs + s_xs + s_ys + s_zs)

    def send_p(h):
        total = psum[h, pl.ds(near * SL, SL)]
        for d in (1, 7, 2, 6, 3, 5, 4):
            other = (z + d) % NZ
            await_part(rsb.at[h, other], rs_recv.at[h, other])
            total = total + rsb[h, other]
        prow[h, own_rows] = total
        spread(prow.at[h, own_rows], pcol, p_send, p_recv, h, True)

    def send_row(h):
        part = prow.at[h, own_rows]
        for d in FAR:
            begin(remote(part, part, pr_send.at[h, d], pr_recv.at[h, z], z_line(d)))

    def s_sum():
        await_part(sswap, sw_recv.at[2])
        ssum[...] = sloc[pl.ds(k * 128, 128)] + sswap[...]
        for cp in s_rs:
            cp.start()

    def s_x():
        for d in FAR:
            other = (z + d) % NZ
            await_part(srs.at[other], sr_recv.at[other])
        total = ssum[pl.ds(z * GS, GS)]
        for d in range(1, NZ):
            total = total + srs[(z + d) % NZ]
        sx[pl.ds(x * GS, GS)] = total
        for cp in s_xs:
            cp.start()

    def s_y():
        sy[pl.ds(y * GS, GS)] = fold_line(sx, x, sx_recv, NX)
        for cp in s_ys:
            cp.start()

    def s_z():
        smat[pl.ds(mine * GS, GS)] = fold_line(sy, y, sy_recv, NY)
        for cp in s_zs:
            cp.start()

    def s_twin():
        await_z(smat, GS, sz_recv)
        s_share.start()

    def on_core(core, step):
        @pl.when(k == core)
        def _():
            step()

    begin_p(0)
    sum_p(0)
    on_core(0, s_sum)
    begin_p(1)
    sum_p(1)
    on_core(1, s_sum)
    await_z(gram, GS, gz_recv)
    to_twin(gram, 128, 3)

    send_p(0)
    on_core(0, s_x)

    await_twin(gram, 128, 3)
    ri = lax.broadcasted_iota(jnp.int32, (NB, NB), 0)
    ci = lax.broadcasted_iota(jnp.int32, (NB, NB), 1)
    ident = jnp.where(ri == ci, 1.0, 0.0).astype(F32)
    full = gram[...]
    diag = jnp.where(ri == ci, full, 0.0) * 0.5
    inv_col = 1.0 / jnp.sum(diag, axis=1, keepdims=True)
    inv_row = 1.0 / jnp.sum(diag, axis=0, keepdims=True)
    strict = jnp.where(ri < ci, full, 0.0) * inv_col
    mid = NB // 2
    eye = ident[:mid, :mid]
    blocks = []
    for b in (slice(0, mid), slice(mid, NB)):
        blocks.append([eye - strict[b, b], dot_full(strict[b, b], strict[b, b], NN)])
    span = 2
    while span < mid:
        for pair in blocks:
            result, power = pair
            pair[0] = result + dot_full(result, power, NN)
            if 2 * span < mid:
                pair[1] = dot_full(power, power, NN)
        span = span * 2
    first, second = blocks[0][0], blocks[1][0]
    corner = -dot_full(dot_full(first, strict[:mid, mid:], NN), second, NN)
    res[:mid] = jnp.concatenate([first, corner], axis=1) * inv_row
    res[mid:] = jnp.concatenate([jnp.zeros((mid, mid), F32), second], axis=1) * inv_row

    on_core(0, s_y)
    send_p(1)
    on_core(1, s_x)
    send_row(0)
    send_row(1)

    tfac = split(res[...])
    high, low = split(dot_split(split(vm[...]), tfac, NT))
    vrh[...] = high
    vrl[...] = low

    def wide_cols(i, carry):
        rows = pl.ds(pl.multiple_of(i * 256, 256), 256)
        high, low = split(dot_split((vch[rows], vcl[rows]), tfac, NT))
        wch[rows] = high
        wcl[rows] = low
        return carry

    lax.fori_loop(0, CB // 256, wide_cols, 0)

    hub_step(*p_ring, 0)
    on_core(1, s_y)
    on_core(0, s_z)
    hub_step(*p_ring, 1)
    on_core(1, s_z)
    for h in range(NH):
        for d in FAR:
            other = (z + d) % NZ
            part = prow.at[h, pl.ds((8 * k + (near + d) % NZ) * SL, SL)]
            await_part(part, pr_recv.at[h, other])
    part = prow.at[:, pl.ds(k * half, half)]
    begin(remote(part, part, sw_send.at[4], sw_recv.at[4], twin))

    on_core(0, s_twin)
    for h in range(NH):
        spread(v_slice(h), vcol, v_send, v_recv, h, False)
        spread(prow.at[h, own_rows], pcol, p_send, p_recv, h, False)
    finish(*v_ring)

    def update(from_ref, left, right, rows):
        cols = dot_split(left, right, NT)
        o_ref[:, rows] = from_ref[:, rows] - cols

    def first_part(h, j, q):
        for g in range(q * NG // 2, (q + 1) * NG // 2):
            await_group(pcol, p_recv, h, j, g)
        rows = pl.ds(RB * j + 256 * q, 256)
        left = (vrh[:, chunk(h)], vrl[:, chunk(h)])
        update(o_ref if h else a_ref, left, split(pcol[h, rows]), rows)

    for q in range(2):
        for j in range(2):
            first_part(0, j, q)

    on_core(1, s_twin)

    def last_part():
        finish(*p_ring)
        all_left()
        await_part(prow.at[:, pl.ds((1 - k) * half, half)], sw_recv.at[4])
        s_share.wait_send()
        await_twin(smat, 128, 5)
        inner = dot_split((vrh[...], vrl[...]), split(smat[...]), NN)
        parts = [split(prow[h] - inner[:, chunk(h)]) for h in range(NH)]
        rest = tuple(jnp.concatenate([part[i] for part in parts], axis=1) for i in range(2))
        for i in range(CB // 256):
            rows = pl.ds(256 * i, 256)
            update(o_ref, rest, (wch[rows], wcl[rows]), rows)

    for q in range(2):
        for j in range(2):
            first_part(1, j, q)
        if q == 0:
            last_part()


def per_device(matrix, reflectors):
    vmem = lambda shape, kind=F32: pltpu.VMEM(shape, kind)
    dma = lambda *shape: pltpu.SemaphoreType.DMA(shape)
    return pl.pallas_call(
        kernel,
        out_shape=pltpu.VMEM((RB, CB), F32),
        in_specs=[pl.BlockSpec(memory_space=pltpu.HBM)] * 2,
        out_specs=pl.BlockSpec(memory_space=pltpu.VMEM),
        scratch_shapes=[
            vmem((RB, CB)),
            vmem((RB, NB)),
            vmem((RB, NB)),
            vmem((NH, CB, HB)),
            vmem((RB, CB), BF16),
            vmem((RB, CB), BF16),
            vmem((CB, NB), BF16),
            vmem((CB, NB), BF16),
            vmem((NH, RB, HB)),
            vmem((NH, RB // 2, HB)),
            vmem((NH, RB // 2, HB)),
            vmem((NH, NZ, SL, HB)),
            vmem((NH, RB, HB)),
            vmem((NH, CB, HB)),
            vmem((NB, NB)),
            vmem((NB, NB)),
            vmem((NX * GS, NB)),
            vmem((NY * GS, NB)),
            vmem((NB, NB)),
            vmem((NB // 2, NB)),
            vmem((NB // 2, NB)),
            vmem((NZ, GS, NB)),
            vmem((NB, NB)),
            vmem((NX * GS, NB)),
            vmem((NY * GS, NB)),
            vmem((NB, NB)),
            vmem((RB, NB), BF16),
            vmem((RB, NB), BF16),
            vmem((CB, NB), BF16),
            vmem((CB, NB), BF16),
            vmem((CB, NB), BF16),
            vmem((CB, NB), BF16),
            dma(2),
            dma(NH, NY),
            dma(NH, 2, NG),
            dma(NH, NG, 3),
            dma(NH, NY),
            dma(NH, 2, NG),
            dma(NH, NG, 3),
            dma(6),
            dma(6),
            dma(NH, NZ),
            dma(NH, NZ),
            dma(NH, NZ),
            dma(NH, NZ),
            dma(NX),
            dma(NX),
            dma(NY),
            dma(NY),
            dma(NZ),
            dma(NZ),
            dma(NZ),
            dma(NZ),
            dma(NX),
            dma(NX),
            dma(NY),
            dma(NY),
            dma(NZ),
            dma(NZ),
        ],
        compiler_params=pltpu.CompilerParams(
            collective_id=1, has_side_effects=True, vmem_limit_bytes=60 * 2**20
        ),
        name="two_sided_update",
    )(matrix, reflectors)


def solution(mesh):
    in_specs = (P("row", "col"), P("row", None))
    out_specs = P("row", "col")
    return jax.shard_map(
        per_device, mesh=mesh, in_specs=in_specs, out_specs=out_specs, check_vma=False
    )
```
